128 devices in a mesh: dp: 8 (over z, core), tensor: 16 (over y, x).
Axes of the slice: x: 4, y: 4, z: 4, core: 2. Of those that a mesh axis runs over, the one named last changes fastest.
Arguments:
- h_in: bfloat16 [1024, 8192], P('dp'), may hold values from -6 to 6
- dout: bfloat16 [1024, 8192], P('dp'), may hold values from -6 to 6
- w_gate: bfloat16 [28672, 512], P('tensor'), may hold values from -0.25 to 0.25
- w_up: bfloat16 [28672, 512], P('tensor'), may hold values from -0.25 to 0.25
- w_down: bfloat16 [28672, 512], P('tensor'), may hold values from -0.125 to 0.125
- in_layout: int32 [224, 4], P('tensor'), may hold values from 0 to 63, all different within a row
- out_layout: int32 [224, 4], P('tensor'), may hold values from 0 to 63, all different within a row
Outputs:
- out: bfloat16 [1024, 8192], P('dp', 'tensor')
- dh: bfloat16 [1024, 8192], P('dp', 'tensor')
- grad_gate: float32 [224, 65536], P('tensor', 'dp')
- grad_up: float32 [224, 65536], P('tensor', 'dp')
- grad_down: float32 [224, 65536], P('tensor', 'dp')
The draws below stay inside these ranges and needn't reach their ends.
Inputs may be any that keep to these rules, and one draw needn't show every extreme that they name: `in_layout`: each block row names 4 different blocks; every block is named by some block row. `out_layout`: each block row names 4 different blocks; every block is named by some block row.
All inputs are finite; a program needn't handle non-finite values.
Results may differ from the reference program's by a relative error of at most 0.018.
Values may be sent and summed in bfloat16 or wider, within the bound.
No kernel may reach another device: no remote copies, remote signals or barrier semaphores. Data moves between devices by JAX's collectives and lax.ppermute only.
A program may use at most 128 MiB of HBM per device.

```python
import jax
import jax.numpy as jnp
from jax import lax

D = 8192
FF = 28672
BLK = 128
KB = 4
NBLK = 64
NROW = 224
TOKENS = 1024
N_TENSOR = 16


def shard_levels(stream_key, dims, cuts, low, largest):
    loudness = 1.0
    for axis_at, shards_of in cuts:
        heights = jax.random.uniform(jax.random.fold_in(jax.random.fold_in(stream_key, 6), axis_at), (shards_of,), jnp.float32, low / len(cuts), largest / len(cuts))
        loudness = loudness * jnp.repeat(jnp.exp(heights), dims[axis_at] // shards_of).reshape((-1,) + (1,) * (len(dims) - 1 - axis_at))
    return loudness


def distinct(rng, rows, count, top, lift):
    sequence = jax.random.permutation(jax.random.fold_in(rng, 1), count)
    boost = sequence
    for power in range(3):
        boost = boost * boost // count
    boost = boost * lift // count
    tickets = jax.random.randint(jax.random.fold_in(rng, 2), (rows, count), 0, 4096) + boost
    fixed_rows = jax.random.permutation(jax.random.fold_in(rng, 3), rows)[jnp.arange(count) % rows]
    tickets = jnp.where(jnp.arange(rows)[:, None] == fixed_rows[None, :], 1 << 14, tickets)
    priority = tickets * count + jnp.arange(count)
    return lax.top_k(priority.astype(jnp.int32), top)[1].astype(jnp.int32)


def gaussian(key, extent, deviation, limit, cuts=(), kind=jnp.bfloat16):
    drawn = jax.random.normal(key, extent, jnp.float32) * deviation
    if len(cuts) > 0:
        drawn = shard_levels(key, extent, cuts, -0.22, 0.18) * drawn
    return jnp.clip(drawn, min=-limit, max=limit).astype(kind)


def setup_inputs(seed: int = 0) -> dict:
    keys = jax.random.split(jax.random.key(seed), 8)
    h_in = gaussian(keys[0], (TOKENS, D), 1.0, 6.0, ((0, 8),))
    dout = gaussian(keys[1], (TOKENS, D), 1.0, 6.0, ((0, 8),))
    w_gate = gaussian(keys[2], (FF, KB * BLK), (KB * BLK) ** -0.5, 0.25, ((0, 16),))
    w_up = gaussian(keys[3], (FF, KB * BLK), (KB * BLK) ** -0.5, 0.25, ((0, 16),))
    w_down = gaussian(keys[4], (FF, KB * BLK), (FF * KB * BLK // D) ** -0.5, 0.125, ((0, 16),))
    in_layout = distinct(keys[5], NROW, NBLK, KB, 0)
    out_layout = distinct(keys[6], NROW, NBLK, KB, 0)
    return dict(h_in=h_in, dout=dout, w_gate=w_gate, w_up=w_up, w_down=w_down, in_layout=in_layout, out_layout=out_layout)


def rounded(value):
    return lax.optimization_barrier(value.astype(jnp.bfloat16))


def reference(h_in, dout, w_gate, w_up, w_down, in_layout, out_layout):
    rows_grp = NROW // N_TENSOR
    tokens = h_in.shape[0]
    nblocks = D // BLK
    h_three = h_in.reshape(tokens, nblocks, BLK)
    d_three = dout.reshape(tokens, nblocks, BLK)
    wg_all = w_gate.reshape(N_TENSOR, rows_grp, BLK, KB * BLK)
    wu_all = w_up.reshape(N_TENSOR, rows_grp, BLK, KB * BLK)
    wd_all = w_down.reshape(N_TENSOR, rows_grp, BLK, KB * BLK)
    lin_all = in_layout.reshape(N_TENSOR, rows_grp * KB).astype(jnp.int32)
    lout_all = out_layout.reshape(N_TENSOR, rows_grp * KB).astype(jnp.int32)

    def one_group(carry, pieces):
        wg_s, wu_s, wd_s, lin_s, lout_s = pieces
        wgf = wg_s.astype(jnp.float32)
        wuf = wu_s.astype(jnp.float32)
        wdf = wd_s.astype(jnp.float32)
        hx_f = jnp.take(h_three, lin_s, axis=1).reshape(tokens, rows_grp, KB * BLK).astype(jnp.float32)
        gate = jnp.einsum('trm,rim->tri', hx_f, wgf)
        up = jnp.einsum('trm,rim->tri', hx_f, wuf)
        sig = jax.nn.sigmoid(gate)
        act = gate * sig
        hidden_f = rounded(act * up).astype(jnp.float32)
        contrib = jnp.einsum('tri,rim->trm', hidden_f, wdf).reshape(tokens, rows_grp * KB, BLK)
        part = jnp.zeros((tokens, nblocks, BLK), jnp.float32).at[:, lout_s].add(contrib)
        out_acc = carry[0] + rounded(part).astype(jnp.float32)
        dob_f = jnp.take(d_three, lout_s, axis=1).reshape(tokens, rows_grp, KB * BLK).astype(jnp.float32)
        dhid = jnp.einsum('trm,rim->tri', dob_f, wdf)
        dgate_f = rounded(dhid * up * sig * (1.0 + gate * (1.0 - sig))).astype(jnp.float32)
        dup_f = rounded(dhid * act).astype(jnp.float32)
        g_down = jnp.einsum('tri,trm->rim', hidden_f, dob_f)
        g_gate = jnp.einsum('tri,trm->rim', dgate_f, hx_f)
        g_up = jnp.einsum('tri,trm->rim', dup_f, hx_f)
        dhx = jnp.einsum('tri,rim->trm', dgate_f, wgf) + jnp.einsum('tri,rim->trm', dup_f, wuf)
        dpart = jnp.zeros((tokens, nblocks, BLK), jnp.float32).at[:, lin_s].add(dhx.reshape(tokens, rows_grp * KB, BLK))
        dh_acc = carry[1] + rounded(dpart).astype(jnp.float32)
        return (out_acc, dh_acc), (g_gate, g_up, g_down)

    start = (jnp.zeros((tokens, nblocks, BLK), jnp.float32), jnp.zeros((tokens, nblocks, BLK), jnp.float32))
    (out_acc, dh_acc), (g_gate, g_up, g_down) = lax.scan(one_group, start, (wg_all, wu_all, wd_all, lin_all, lout_all))
    out = out_acc.reshape(tokens, D).astype(jnp.bfloat16)
    dh = dh_acc.reshape(tokens, D).astype(jnp.bfloat16)
    width = BLK * KB * BLK
    return (out, dh, g_gate.reshape(NROW, width), g_up.reshape(NROW, width), g_down.reshape(NROW, width))
```

```python
import jax
import jax.numpy as jnp
from jax import lax
from jax.experimental import pallas as pl
from jax.experimental.pallas import tpu as pltpu
from jax.sharding import PartitionSpec as P

D = 8192
BLK = 128
KB = 4
W = KB * BLK
NBLK = D // BLK
ROWS = 14
TOK = 128
AXES = ("dp", "tensor")
F32 = jnp.float32
BF16 = jnp.bfloat16
NT = (((1,), (1,)), ((), ()))


def pairs(axis, step):
    out = []
    for d in range(128):
        dp, t = divmod(d, 16)
        z, c = divmod(dp, 2)
        y, x = divmod(t, 4)
        m = 1 if (c == 0) == (step == 0) else 3
        if axis == "x":
            x ^= m
        elif axis == "y":
            y ^= m
        elif axis == "z":
            z ^= m
        else:
            c ^= 1
        out.append((d, (z * 2 + c) * 16 + y * 4 + x))
    return out


def send(a, axis, step=0):
    return lax.ppermute(a, AXES, pairs(axis, step))


def ring_order(me, core):
    first = 1 + 2 * core
    return (me ^ first, me ^ 2, me, me ^ (first ^ 2))


def dot(a, b, dims=None):
    if dims is None:
        return jnp.dot(a, b, preferred_element_type=F32)
    return lax.dot_general(a, b, dims, preferred_element_type=F32)


def gather_cols(ref, lay, r):
    return jnp.concatenate(
        [ref[:, pl.ds(pl.multiple_of(lay[r, k] * BLK, BLK), BLK)] for k in range(KB)], axis=1
    )


def split_units(pos, act, tmp, keep, give, a, wide):
    z, c = pos[0], pos[1]
    tmp[...] = act.T.reshape(8, 16, TOK)
    for q, own in enumerate(ring_order(z, c)):
        keep[a, 0, q] = tmp[own * 2 + c]
    for q, own in enumerate(ring_order(z, 1 - c)):
        give[a, 0, q] = tmp[own * 2 + 1 - c]


def emit_chunks(acc, outer, inner, transposed, sent, kept):
    for p in range(4):
        dst = sent if p < 2 else kept
        for q in range(4):
            y, x = (inner[q], outer[p]) if transposed else (outer[p], inner[q])
            base = (y * 4 + x) * 4
            for j in range(4):
                dst[p % 2, q, :, j * BLK : (j + 1) * BLK] = acc[base + j].astype(BF16)


def forward_kernel(pos, lin, lout, h, wg, wu, wd, a_out, b_out, keep, give, sent, kept, acc, tmp):
    r = pl.program_id(0)

    @pl.when(r == 0)
    def _():
        acc[...] = jnp.zeros_like(acc)

    hx = gather_cols(h, lin, r)
    gate = dot(hx, wg[...], NT)
    up = dot(hx, wu[...], NT)
    sig = jax.nn.sigmoid(gate)
    silu = gate * sig
    hidden = (silu * up).astype(BF16)
    a_out[0] = up * sig * (1.0 + gate * (1.0 - sig))
    b_out[0] = silu
    part = dot(hidden, wd[...])
    for k in range(KB):
        acc[lout[r, k]] += part[:, k * BLK : (k + 1) * BLK]
    split_units(pos, hidden, tmp, keep, give, 0, 1)

    @pl.when(r == ROWS - 1)
    def _():
        xs, ys = ring_order(pos[3], pos[1]), ring_order(pos[2], pos[1])
        emit_chunks(acc, xs, ys, True, sent, kept)


def backward_kernel(pos, lin, lout, dout, wg, wu, wd, a_in, b_in, keep, give, sent, kept, acc, tmp):
    r = pl.program_id(0)

    @pl.when(r == 0)
    def _():
        acc[...] = jnp.zeros_like(acc)

    dob = gather_cols(dout, lout, r)
    dhid = dot(dob, wd[...], NT)
    dgate = (dhid * a_in[0]).astype(BF16)
    dup = (dhid * b_in[0]).astype(BF16)
    part = dot(dgate, wg[...]) + dot(dup, wu[...])
    for k in range(KB):
        acc[lin[r, k]] += part[:, k * BLK : (k + 1) * BLK]
    split_units(pos, dgate, tmp, keep, give, 0, 2)
    split_units(pos, dup, tmp, keep, give, 1, 2)

    @pl.when(r == ROWS - 1)
    def _():
        xs, ys = ring_order(pos[3], pos[1]), ring_order(pos[2], pos[1])
        emit_chunks(acc, ys, xs, False, sent, kept)


def grads_kernel(lin, lout, h0, h1, d0, d1, hid0, hid1, dg0, dg1, sent, kept):
    r = pl.program_id(0)
    hx = jnp.concatenate([gather_cols(h0, lin, r), gather_cols(h1, lin, r)], axis=0)
    dob = jnp.concatenate([gather_cols(d0, lout, r), gather_cols(d1, lout, r)], axis=0)
    hid = jnp.concatenate([hid0[...].reshape(64, TOK), hid1[...].reshape(64, TOK)], axis=1)
    dgu = jnp.concatenate([dg0[...].reshape(128, TOK), dg1[...].reshape(128, TOK)], axis=1)
    g_in = dot(dgu, hx).astype(BF16).reshape(2, 4, 16, W)
    g_down = dot(hid, dob).astype(BF16).reshape(4, 16, W)
    for q in range(4):
        dst = sent if q < 2 else kept
        dst[q % 2, 0, 0] = g_in[0, q]
        dst[q % 2, 1, 0] = g_in[1, q]
        dst[q % 2, 2, 0] = g_down[q]


def finish_kernel(own, r1, r2, gate, up, down, tmp):
    for g, out in enumerate((gate, up, down)):
        total = own[0, g].astype(F32) + r1[0, g].astype(F32) + r2[g].astype(F32)
        total = total.reshape(ROWS * 16, W)
        for k in range(KB):
            tmp[k] = total[:, k * BLK : (k + 1) * BLK]
        for i in range(16):
            for k in range(KB):
                at = i * W + k * BLK
                out[:, at : at + BLK] = tmp[k, pl.ds(i, ROWS, stride=16), :]


def const(*shape):
    return pl.BlockSpec(shape, lambda r, *_: (0,) * len(shape))


def per_row(*shape, at=0):
    return pl.BlockSpec(shape, lambda r, *_: tuple(r if d == at else 0 for d in range(len(shape))))


PARAMS = pltpu.CompilerParams(vmem_limit_bytes=48 * 2**20, dimension_semantics=("arbitrary",))


def pass_call(kernel, n_act, tokens, ops, args, extra_in, extra_out):
    act = jax.ShapeDtypeStruct((n_act, ROWS, 4, 16, TOK), BF16)
    chunks = jax.ShapeDtypeStruct((2, 4, TOK, W), BF16)
    act_spec = per_row(n_act, 1, 4, 16, TOK, at=1)
    return pl.pallas_call(
        kernel,
        grid_spec=pltpu.PrefetchScalarGridSpec(
            num_scalar_prefetch=3,
            grid=(ROWS,),
            in_specs=[const(TOK, D)] + [per_row(BLK, W)] * 3 + [per_row(1, BLK, BLK)] * extra_in,
            out_specs=[per_row(1, TOK, BLK)] * extra_out
            + [act_spec, act_spec, const(2, 4, TOK, W), const(2, 4, TOK, W)],
            scratch_shapes=[pltpu.VMEM((NBLK, TOK, BLK), F32), pltpu.VMEM((8, 16, TOK), BF16)],
        ),
        out_shape=[jax.ShapeDtypeStruct((ROWS, TOK, BLK), F32)] * extra_out + [act, act, chunks, chunks],
        compiler_params=PARAMS,
        cost_estimate=pl.CostEstimate(
            flops=3 * 2 * TOK * ROWS * BLK * W, bytes_accessed=16 * 2**20, transcendentals=0
        ),
    )(*args)


def grads_call(lin, lout, h0, h1, d0, d1, hid0, hid1, dg0, dg1):
    out = jax.ShapeDtypeStruct((2, 3, ROWS, 16, W), BF16)
    return pl.pallas_call(
        grads_kernel,
        grid_spec=pltpu.PrefetchScalarGridSpec(
            num_scalar_prefetch=2,
            grid=(ROWS,),
            in_specs=[const(TOK, D)] * 4
            + [per_row(1, 1, 4, 16, TOK, at=1)] * 2
            + [per_row(2, 1, 4, 16, TOK, at=1)] * 2,
            out_specs=[per_row(2, 3, 1, 16, W, at=2)] * 2,
        ),
        out_shape=[out, out],
        compiler_params=PARAMS,
        cost_estimate=pl.CostEstimate(
            flops=3 * 2 * TOK * ROWS * BLK * W, bytes_accessed=16 * 2**20, transcendentals=0
        ),
    )(lin, lout, h0, h1, d0, d1, hid0, hid1, dg0, dg1)


def finish_call(own, r1, r2):
    out = jax.ShapeDtypeStruct((ROWS, 16 * W), F32)
    first = pl.BlockSpec((1, 3, ROWS, 16, W), lambda i: (0, 0, 0, 0, 0))
    return pl.pallas_call(
        finish_kernel,
        grid=(1,),
        in_specs=[first, first, pl.BlockSpec((3, ROWS, 16, W), lambda i: (0, 0, 0, 0))],
        out_specs=[pl.BlockSpec((ROWS, 16 * W), lambda i: (0, 0))] * 3,
        out_shape=[out] * 3,
        scratch_shapes=[pltpu.VMEM((KB, ROWS * 16, BLK), F32)],
        compiler_params=PARAMS,
    )(own, r1, r2)


def add(*terms):
    return sum(t.astype(F32) for t in terms).astype(BF16)


def ring_pair(sent, kept, first, second):
    r1 = send(sent, first, 0)
    r2 = send(add(kept[1], r1[1]), first, 1)
    mid = add(kept[0], r1[0], r2)
    r3 = send(mid[0:2], second, 0)
    r4 = send(add(mid[3], r3[1]), second, 1)
    return add(mid[2], r3[0], r4)


def shards(h_in, dout, w_gate, w_up, w_down, in_layout, out_layout):
    dp, t = lax.axis_index("dp"), lax.axis_index("tensor")
    pos = jnp.stack([dp // 2, dp % 2, t // 4, t % 4]).astype(jnp.int32)
    h_other = send(h_in, "core")
    d_other = send(dout, "core")
    a, b, hid_keep, hid_give, p_sent, p_kept = pass_call(
        forward_kernel, 1, TOK, None, (pos, in_layout, out_layout, h_in, w_gate, w_up, w_down), 0, 2
    )
    dg_keep, dg_give, q_sent, q_kept = pass_call(
        backward_kernel, 2, TOK, None, (pos, in_layout, out_layout, dout, w_gate, w_up, w_down, a, b), 2, 0
    )
    hid_other = send(hid_give, "core")
    dg_other = send(dg_give, "core")
    g_sent, g_kept = grads_call(
        in_layout, out_layout, h_in, h_other, dout, d_other, hid_keep, hid_other, dg_keep, dg_other
    )
    g1 = send(g_sent, "z", 0)
    g2 = send(add(g_kept[1], g1[1]), "z", 1)
    g_gate, g_up, g_down = finish_call(g_kept, g1, g2)
    out = ring_pair(p_sent, p_kept, "x", "y")
    dh = ring_pair(q_sent, q_kept, "y", "x")
    return (out, dh, g_gate, g_up, g_down)


def solution(mesh):
    rows = P("tensor", None)
    return jax.shard_map(
        shards,
        mesh=mesh,
        in_specs=(P("dp", None), P("dp", None), rows, rows, rows, rows, rows),
        out_specs=(P("dp", "tensor"), P("dp", "tensor")) + (P("tensor", "dp"),) * 3,
        check_vma=False,
    )
```

```python
import jax
import jax.numpy as jnp
from jax import lax
from jax.experimental import pallas as pl
from jax.experimental.pallas import tpu as pltpu
from jax.sharding import PartitionSpec as P

D = 8192
BLK = 128
KB = 4
W = KB * BLK
NBLK = D // BLK
ROWS = 14
TOK = 128
AXES = ("dp", "tensor")
F32 = jnp.float32
BF16 = jnp.bfloat16
NT = (((1,), (1,)), ((), ()))


def pairs(axis, step):
    out = []
    for d in range(128):
        dp, t = divmod(d, 16)
        z, c = divmod(dp, 2)
        y, x = divmod(t, 4)
        m = 1 if (c == 0) == (step == 0) else 3
        if axis == "x":
            x ^= m
        elif axis == "y":
            y ^= m
        elif axis == "z":
            z ^= m
        else:
            c ^= 1
        out.append((d, (z * 2 + c) * 16 + y * 4 + x))
    return out


def send(a, axis, step=0):
    return lax.ppermute(a, AXES, pairs(axis, step))


def ring_order(me, core):
    first = 1 + 2 * core
    return (me ^ first, me ^ 2, me, me ^ (first ^ 2))


def dot(a, b, dims=None):
    if dims is None:
        return jnp.dot(a, b, preferred_element_type=F32)
    return lax.dot_general(a, b, dims, preferred_element_type=F32)


def gather_cols(ref, lay, r):
    return jnp.concatenate(
        [ref[:, pl.ds(pl.multiple_of(lay[r, k] * BLK, BLK), BLK)] for k in range(KB)], axis=1
    )


def emit_chunks(acc, outer, inner, transposed, sent, kept):
    for p in range(4):
        dst = sent if p < 2 else kept
        for q in range(4):
            y, x = (inner[q], outer[p]) if transposed else (outer[p], inner[q])
            base = (y * 4 + x) * 4
            for j in range(4):
                dst[p % 2, q, :, j * BLK : (j + 1) * BLK] = acc[base + j].astype(BF16)


def main_kernel(
    pos, lin_hbm, lout_hbm, h_hbm, d_hbm, wg_hbm, wu_hbm, wd_hbm,
    keep, give, p_sent, p_kept, q_sent, q_kept, h, d,
    wg, wu, wd, acc_p, acc_q, hid, dgu, turned, lin, lout, sem, w_sem,
):
    small = [
        pltpu.make_async_copy(lin_hbm, lin, sem.at[0]),
        pltpu.make_async_copy(lout_hbm, lout, sem.at[1]),
        pltpu.make_async_copy(h_hbm, h, sem.at[2]),
        pltpu.make_async_copy(d_hbm, d, sem.at[3]),
    ]

    def weights(start, n):
        rows = pl.ds(start * BLK, n * BLK)
        both = ((wg_hbm, wg), (wu_hbm, wu), (wd_hbm, wd))
        return [
            pltpu.make_async_copy(src.at[rows], dst.at[rows], w_sem.at[i, 0 if start == 0 else 1])
            for i, (src, dst) in enumerate(both)
        ]

    early, late = weights(0, EARLY), weights(EARLY, ROWS - EARLY)
    for c in small + early + late:
        c.start()
    acc_p[...] = jnp.zeros_like(acc_p)
    acc_q[...] = jnp.zeros_like(acc_q)
    for c in small + early:
        c.wait()
    z, core = pos[0], pos[1]
    mine = [o * 2 + core for o in ring_order(z, core)]
    others = [o * 2 + 1 - core for o in ring_order(z, 1 - core)]

    def rows_of(r):
        at = r * BLK if isinstance(r, int) else pl.multiple_of(r * BLK, BLK)
        return pl.ds(at, BLK)

    def units(s):
        for i in range(UNROLL):
            r = s * UNROLL + i
            sl = rows_of(r)
            hx, dob = gather_cols(h, lin, r), gather_cols(d, lout, r)
            gate, up, dhid = dot(hx, wg[sl], NT), dot(hx, wu[sl], NT), dot(dob, wd[sl], NT)
            sig = jax.nn.sigmoid(gate)
            silu = gate * sig
            hidden = (silu * up).astype(BF16)
            dgate = (dhid * up * sig * (1.0 + gate * (1.0 - sig))).astype(BF16)
            dup = (dhid * silu).astype(BF16)
            hid[r] = hidden
            dgu[r, :, :BLK] = dgate
            dgu[r, :, BLK:] = dup
            for a, v in enumerate((hidden, dgate, dup)):
                turned[r, a] = v.T.reshape(8, 16, TOK)

    def features(s):
        for i in range(UNROLL):
            r = s * UNROLL + i
            sl = rows_of(r)
            part = dot(hid[r], wd[sl])
            dhx = dot(dgu[r], jnp.concatenate([wg[sl], wu[sl]], axis=0))
            for k in range(KB):
                acc_p[lout[r, k]] += part[:, k * BLK : (k + 1) * BLK]
            for k in range(KB):
                acc_q[lin[r, k]] += dhx[:, k * BLK : (k + 1) * BLK]
            for a in range(3):
                for q in range(4):
                    keep[a, r, q] = turned[r, a, mine[q]]
                    give[a, r, q] = turned[r, a, others[q]]

    def both(s):
        features(s - 1)
        units(s)

    units(0)
    pl.loop(1, EARLY // UNROLL)(both)
    for c in late:
        c.wait()
    pl.loop(EARLY // UNROLL, ROWS // UNROLL)(both)
    features(ROWS // UNROLL - 1)
    xs, ys = ring_order(pos[3], core), ring_order(pos[2], core)
    emit_chunks(acc_p, xs, ys, True, p_sent, p_kept)
    emit_chunks(acc_q, ys, xs, False, q_sent, q_kept)


def grads_kernel(lin, lout, h0, h1, d0, d1, act0, act1, sent, kept):
    @pl.loop(0, ROWS // UNROLL)
    def _(s):
        for i in range(UNROLL):
            r = s * UNROLL + i
            hx = jnp.concatenate([gather_cols(h0, lin, r), gather_cols(h1, lin, r)], axis=0)
            dob = jnp.concatenate([gather_cols(d0, lout, r), gather_cols(d1, lout, r)], axis=0)
            act = [
                jnp.concatenate([act0[a, r].reshape(64, TOK), act1[a, r].reshape(64, TOK)], axis=1)
                for a in range(3)
            ]
            g_in = dot(jnp.concatenate(act[1:], axis=0), hx).astype(BF16).reshape(2, 4, 16, W)
            g_down = dot(act[0], dob).astype(BF16).reshape(4, 16, W)
            for q in range(4):
                dst = sent if q < 2 else kept
                dst[q % 2, 0, r] = g_in[0, q]
                dst[q % 2, 1, r] = g_in[1, q]
                dst[q % 2, 2, r] = g_down[q]


def finish_kernel(own, r1, r2, gate, up, down, tmp):
    for g, out in enumerate((gate, up, down)):
        total = own[0, g].astype(F32) + r1[0, g].astype(F32) + r2[g].astype(F32)
        total = total.reshape(ROWS * 16, W)
        for k in range(KB):
            tmp[k] = total[:, k * BLK : (k + 1) * BLK]
        for i in range(16):
            for k in range(KB):
                at = i * W + k * BLK
                out[:, at : at + BLK] = tmp[k, pl.ds(i, ROWS, stride=16), :]


V = pltpu.VMEM
IN_SMEM = pl.BlockSpec(memory_space=pltpu.SMEM)
IN_VMEM = pl.BlockSpec(memory_space=pltpu.VMEM)
ANYWHERE = pl.BlockSpec(memory_space=pl.ANY)
UNROLL = 2
EARLY = 4


def in_hbm(*arrays):
    return [pltpu.with_memory_space_constraint(a, pltpu.HBM) for a in arrays]


def in_vmem(*arrays):
    return [pltpu.with_memory_space_constraint(a, pltpu.VMEM) for a in arrays]


def cost(mib):
    return pl.CostEstimate(flops=10**9, bytes_accessed=mib * 2**20, transcendentals=0)


def main_call(pos, *arrays):
    act = V((3, ROWS, 4, 16, TOK), BF16)
    chunks = V((2, 4, TOK, W), BF16)
    weight = V((ROWS * BLK, W), BF16)
    total = V((NBLK, TOK, BLK), F32)
    layout = pltpu.SMEM((ROWS, KB), jnp.int32)
    return pl.pallas_call(
        main_kernel,
        in_specs=[IN_SMEM] + [ANYWHERE] * 7,
        out_specs=[IN_VMEM] * 8,
        out_shape=[act, act, chunks, chunks, chunks, chunks, V((TOK, D), BF16), V((TOK, D), BF16)],
        scratch_shapes=[
            weight, weight, weight, total, total,
            V((ROWS, TOK, BLK), BF16), V((ROWS, TOK, 2 * BLK), BF16), V((ROWS, 3, 8, 16, TOK), BF16),
            layout, layout, pltpu.SemaphoreType.DMA((4,)), pltpu.SemaphoreType.DMA((3, 2)),
        ],
        compiler_params=pltpu.CompilerParams(vmem_limit_bytes=24 * 2**20),
        cost_estimate=cost(24),
    )(pos, *in_hbm(*arrays))


def grads_call(lin, lout, *arrays):
    out = V((2, 3, ROWS, 16, W), BF16)
    return pl.pallas_call(
        grads_kernel,
        in_specs=[IN_SMEM] * 2 + [IN_VMEM] * 6,
        out_specs=[IN_VMEM] * 2,
        out_shape=[out, out],
        compiler_params=pltpu.CompilerParams(vmem_limit_bytes=4 * 2**20),
        cost_estimate=cost(12),
    )(lin, lout, *in_vmem(*arrays))


def finish_call(*arrays):
    out = jax.ShapeDtypeStruct((ROWS, 16 * W), F32)
    return pl.pallas_call(
        finish_kernel,
        in_specs=[IN_VMEM] * 3,
        out_specs=[IN_VMEM] * 3,
        out_shape=[out] * 3,
        scratch_shapes=[V((KB, ROWS * 16, BLK), F32)],
        compiler_params=pltpu.CompilerParams(vmem_limit_bytes=8 * 2**20),
        cost_estimate=cost(6),
    )(*in_vmem(*arrays))


def add(*terms):
    return sum(t.astype(F32) for t in terms).astype(BF16)


def ring_pair(sent, kept, first, second):
    r1 = send(sent, first, 0)
    r2 = send(add(kept[1], r1[1]), first, 1)
    mid = add(kept[0], r1[0], r2)
    r3 = send(mid[0:2], second, 0)
    r4 = send(add(mid[3], r3[1]), second, 1)
    return add(mid[2], r3[0], r4)


def shards(h_in, dout, w_gate, w_up, w_down, in_layout, out_layout):
    dp, t = lax.axis_index("dp"), lax.axis_index("tensor")
    pos = jnp.stack([dp // 2, dp % 2, t // 4, t % 4]).astype(jnp.int32)
    h_other = send(h_in, "core")
    d_other = send(dout, "core")
    keep, give, p_sent, p_kept, q_sent, q_kept, h_own, d_own = main_call(
        pos, in_layout, out_layout, h_in, dout, w_gate, w_up, w_down
    )
    taken = send(give, "core")
    g_sent, g_kept = grads_call(in_layout, out_layout, h_own, h_other, d_own, d_other, keep, taken)
    g1 = send(g_sent, "z", 0)
    g2 = send(add(g_kept[1], g1[1]), "z", 1)
    g_gate, g_up, g_down = finish_call(g_kept, g1, g2)
    out = ring_pair(p_sent, p_kept, "x", "y")
    dh = ring_pair(q_sent, q_kept, "y", "x")
    return (out, dh, g_gate, g_up, g_down)


def solution(mesh):
    rows = P("tensor", None)
    return jax.shard_map(
        shards,
        mesh=mesh,
        in_specs=(P("dp", None), P("dp", None), rows, rows, rows, rows, rows),
        out_specs=(P("dp", "tensor"), P("dp", "tensor")) + (P("tensor", "dp"),) * 3,
        check_vma=False,
    )
```

```python
import jax
import jax.numpy as jnp
from jax import lax
from jax.experimental import pallas as pl
from jax.experimental.pallas import tpu as pltpu
from jax.sharding import PartitionSpec as P

D = 8192
BLK = 128
KB = 4
W = KB * BLK
NBLK = D // BLK
ROWS = 14
TOK = 128
AXES = ("dp", "tensor")
F32 = jnp.float32
BF16 = jnp.bfloat16
NT = (((1,), (1,)), ((), ()))


def pairs(axis, step):
    out = []
    for d in range(128):
        dp, t = divmod(d, 16)
        z, c = divmod(dp, 2)
        y, x = divmod(t, 4)
        m = 1 if (c == 0) == (step == 0) else 3
        if axis == "x":
            x ^= m
        elif axis == "y":
            y ^= m
        elif axis == "z":
            z ^= m
        else:
            c ^= 1
        out.append((d, (z * 2 + c) * 16 + y * 4 + x))
    return out


def send(a, axis, step=0):
    return lax.ppermute(a, AXES, pairs(axis, step))


def ring_order(me, core):
    first = 1 + 2 * core
    return (me ^ first, me ^ 2, me, me ^ (first ^ 2))


def dot(a, b, dims=None):
    if dims is None:
        return jnp.dot(a, b, preferred_element_type=F32)
    return lax.dot_general(a, b, dims, preferred_element_type=F32)


def gather_cols(ref, lay, r):
    return jnp.concatenate(
        [ref[:, pl.ds(pl.multiple_of(lay[k, r] * BLK, BLK), BLK)] for k in range(KB)], axis=1
    )


def emit_chunks(acc, outer, inner, transposed, sent, kept):
    for p in range(4):
        dst = sent if p < 2 else kept
        for q in range(4):
            y, x = (inner[q], outer[p]) if transposed else (outer[p], inner[q])
            base = (y * 4 + x) * 4
            for j in range(4):
                dst[p % 2, q, :, j * BLK : (j + 1) * BLK] = acc[base + j].astype(BF16)


def main_kernel(
    pos, lin_hbm, lout_hbm, h_hbm, d_hbm, wg_hbm, wu_hbm, wd_hbm,
    keep, give, p_sent, p_kept, q_sent, q_kept, h, d,
    wg, wu, wd, acc_p, acc_q, hid, dgu, turned, lin, lout, sem, w_sem,
):
    small = [
        pltpu.make_async_copy(lin_hbm, lin, sem.at[0]),
        pltpu.make_async_copy(lout_hbm, lout, sem.at[1]),
        pltpu.make_async_copy(h_hbm, h, sem.at[2]),
        pltpu.make_async_copy(d_hbm, d, sem.at[3]),
    ]

    def weights(start, n):
        rows = pl.ds(start * BLK, n * BLK)
        both = ((wg_hbm, wg), (wu_hbm, wu), (wd_hbm, wd))
        return [
            pltpu.make_async_copy(src.at[rows], dst.at[rows], w_sem.at[i, 0 if start == 0 else 1])
            for i, (src, dst) in enumerate(both)
        ]

    early, late = weights(0, EARLY), weights(EARLY, ROWS - EARLY)
    for c in small + early + late:
        c.start()
    acc_p[...] = jnp.zeros_like(acc_p)
    acc_q[...] = jnp.zeros_like(acc_q)
    for c in small + early:
        c.wait()
    z, core = pos[0], pos[1]
    mine = [o * 2 + core for o in ring_order(z, core)]
    others = [o * 2 + 1 - core for o in ring_order(z, 1 - core)]

    def rows_of(r):
        at = r * BLK if isinstance(r, int) else pl.multiple_of(r * BLK, BLK)
        return pl.ds(at, BLK)

    def units(s):
        for i in range(UNROLL):
            r = s * UNROLL + i
            sl = rows_of(r)
            hx, dob = gather_cols(h, lin, r), gather_cols(d, lout, r)
            gate, up, dhid = dot(hx, wg[sl], NT), dot(hx, wu[sl], NT), dot(dob, wd[sl], NT)
            sig = jax.nn.sigmoid(gate)
            silu = gate * sig
            hidden = (silu * up).astype(BF16)
            dgate = (dhid * up * sig * (1.0 + gate * (1.0 - sig))).astype(BF16)
            dup = (dhid * silu).astype(BF16)
            hid[r] = hidden
            dgu[r, :, :BLK] = dgate
            dgu[r, :, BLK:] = dup
            for a, v in enumerate((hidden, dgate, dup)):
                turned[r, a] = v.T.reshape(8, 16, TOK)

    def features(s):
        for i in range(UNROLL):
            r = s * UNROLL + i
            sl = rows_of(r)
            part = dot(hid[r], wd[sl])
            dhx = dot(dgu[r], jnp.concatenate([wg[sl], wu[sl]], axis=0))
            for k in range(KB):
                acc_p[lout[k, r]] += part[:, k * BLK : (k + 1) * BLK]
            for k in range(KB):
                acc_q[lin[k, r]] += dhx[:, k * BLK : (k + 1) * BLK]
            for a in range(3):
                for q in range(4):
                    keep[a, r, q] = turned[r, a, mine[q]]
                    give[a, r, q] = turned[r, a, others[q]]

    def both(s):
        features(s - 1)
        units(s)

    units(0)
    pl.loop(1, EARLY // UNROLL)(both)
    for c in late:
        c.wait()
    pl.loop(EARLY // UNROLL, ROWS // UNROLL)(both)
    features(ROWS // UNROLL - 1)
    xs, ys = ring_order(pos[3], core), ring_order(pos[2], core)
    emit_chunks(acc_p, xs, ys, True, p_sent, p_kept)
    emit_chunks(acc_q, ys, xs, False, q_sent, q_kept)


def grads_kernel(lin, lout, h0, h1, d0, d1, act0, act1, sent, kept):
    @pl.loop(0, ROWS // UNROLL)
    def _(s):
        for i in range(UNROLL):
            r = s * UNROLL + i
            hx = jnp.concatenate([gather_cols(h0, lin, r), gather_cols(h1, lin, r)], axis=0)
            dob = jnp.concatenate([gather_cols(d0, lout, r), gather_cols(d1, lout, r)], axis=0)
            act = [
                jnp.concatenate([act0[a, r].reshape(64, TOK), act1[a, r].reshape(64, TOK)], axis=1)
                for a in range(3)
            ]
            g_in = dot(jnp.concatenate(act[1:], axis=0), hx).astype(BF16).reshape(2, 4, 16, W)
            g_down = dot(act[0], dob).astype(BF16).reshape(4, 16, W)
            for q in range(4):
                dst = sent if q < 2 else kept
                dst[q % 2, 0, r] = g_in[0, q]
                dst[q % 2, 1, r] = g_in[1, q]
                dst[q % 2, 2, r] = g_down[q]


def finish_kernel(own, r1, r2, gate, up, down, tmp):
    for g, out in enumerate((gate, up, down)):
        total = own[0, g].astype(F32) + r1[0, g].astype(F32) + r2[g].astype(F32)
        total = total.reshape(ROWS * 16, W)
        for k in range(KB):
            tmp[k] = total[:, k * BLK : (k + 1) * BLK]
        for i in range(16):
            for k in range(KB):
                at = i * W + k * BLK
                out[:, at : at + BLK] = tmp[k, pl.ds(i, ROWS, stride=16), :]


V = pltpu.VMEM
IN_SMEM = pl.BlockSpec(memory_space=pltpu.SMEM)
IN_VMEM = pl.BlockSpec(memory_space=pltpu.VMEM)
ANYWHERE = pl.BlockSpec(memory_space=pl.ANY)
UNROLL = 2
EARLY = 4


def in_hbm(*arrays):
    return [pltpu.with_memory_space_constraint(a, pltpu.HBM) for a in arrays]


def in_vmem(*arrays):
    return [pltpu.with_memory_space_constraint(a, pltpu.VMEM) for a in arrays]


def cost(mib):
    return pl.CostEstimate(flops=10**9, bytes_accessed=mib * 2**20, transcendentals=0)


def main_call(pos, *arrays):
    act = V((3, ROWS, 4, 16, TOK), BF16)
    chunks = V((2, 4, TOK, W), BF16)
    weight = V((ROWS * BLK, W), BF16)
    total = V((NBLK, TOK, BLK), F32)
    layout = pltpu.SMEM((KB, ROWS), jnp.int32)
    return pl.pallas_call(
        main_kernel,
        in_specs=[IN_SMEM] + [ANYWHERE] * 7,
        out_specs=[IN_VMEM] * 8,
        out_shape=[act, act, chunks, chunks, chunks, chunks, V((TOK, D), BF16), V((TOK, D), BF16)],
        scratch_shapes=[
            weight, weight, weight, total, total,
            V((ROWS, TOK, BLK), BF16), V((ROWS, TOK, 2 * BLK), BF16), V((ROWS, 3, 8, 16, TOK), BF16),
            layout, layout, pltpu.SemaphoreType.DMA((4,)), pltpu.SemaphoreType.DMA((3, 2)),
        ],
        compiler_params=pltpu.CompilerParams(vmem_limit_bytes=24 * 2**20),
        cost_estimate=cost(24),
    )(pos, *in_hbm(*arrays))


def grads_call(lin, lout, *arrays):
    out = V((2, 3, ROWS, 16, W), BF16)
    return pl.pallas_call(
        grads_kernel,
        in_specs=[IN_SMEM] * 2 + [IN_VMEM] * 6,
        out_specs=[IN_VMEM] * 2,
        out_shape=[out, out],
        compiler_params=pltpu.CompilerParams(vmem_limit_bytes=4 * 2**20),
        cost_estimate=cost(12),
    )(lin, lout, *in_vmem(*arrays))


def finish_call(*arrays):
    out = jax.ShapeDtypeStruct((ROWS, 16 * W), F32)
    return pl.pallas_call(
        finish_kernel,
        in_specs=[IN_VMEM] * 3,
        out_specs=[IN_VMEM] * 3,
        out_shape=[out] * 3,
        scratch_shapes=[V((KB, ROWS * 16, BLK), F32)],
        compiler_params=pltpu.CompilerParams(vmem_limit_bytes=8 * 2**20),
        cost_estimate=cost(6),
    )(*in_vmem(*arrays))


def add(*terms):
    return sum(t.astype(F32) for t in terms).astype(BF16)


def after(value, other):
    return lax.optimization_barrier((value, other))[0]


def shards(h_in, dout, w_gate, w_up, w_down, in_layout, out_layout):
    in_layout, out_layout = in_layout.T, out_layout.T
    dp, t = lax.axis_index("dp"), lax.axis_index("tensor")
    pos = jnp.stack([dp // 2, dp % 2, t // 4, t % 4]).astype(jnp.int32)
    h_other = send(h_in, "core")
    d_other = send(dout, "core")
    keep, give, p_sent, p_kept, q_sent, q_kept, h_own, d_own = main_call(
        pos, in_layout, out_layout, h_in, dout, w_gate, w_up, w_down
    )
    taken = send(give, "core")
    g_sent, g_kept = grads_call(in_layout, out_layout, h_own, h_other, d_own, d_other, keep, taken)
    p1, q1 = send(p_sent, "x", 0), send(q_sent, "y", 0)
    g1 = send(g_sent, "z", 0)
    p2 = send(add(p_kept[1], p1[1]), "x", 1)
    q2 = send(add(q_kept[1], q1[1]), "y", 1)
    p_mid = add(p_kept[0], p1[0], p2)
    p3 = send(p_mid[0:2], "y", 0)
    g_half = add(g_kept[1], after(g1, p_mid)[1])
    g2 = send(g_half, "z", 1)
    q_mid = add(q_kept[0], q1[0], after(q2, g_half))
    q3 = send(q_mid[0:2], "x", 0)
    p4 = send(add(p_mid[3], p3[1]), "y", 1)
    q4 = send(add(q_mid[3], q3[1]), "x", 1)
    g_gate, g_up, g_down = finish_call(g_kept, g1, g2)
    out = add(p_mid[2], p3[0], after(p4, g_gate))
    dh = add(q_mid[2], q3[0], after(q4, g_gate))
    return (out, dh, g_gate, g_up, g_down)


def solution(mesh):
    rows = P("tensor", None)
    return jax.shard_map(
        shards,
        mesh=mesh,
        in_specs=(P("dp", None), P("dp", None), rows, rows, rows, rows, rows),
        out_specs=(P("dp", "tensor"), P("dp", "tensor")) + (P("tensor", "dp"),) * 3,
        check_vma=False,
    )
```

```python
import jax
import jax.numpy as jnp
from jax import lax
from jax.experimental import pallas as pl
from jax.experimental.pallas import tpu as pltpu
from jax.sharding import PartitionSpec as P

D = 8192
BLK = 128
KB = 4
W = KB * BLK
NBLK = D // BLK
ROWS = 14
TOK = 128
AXES = ("dp", "tensor")
F32 = jnp.float32
BF16 = jnp.bfloat16
NT = (((1,), (1,)), ((), ()))


def pairs(axis, step):
    out = []
    for d in range(128):
        dp, t = divmod(d, 16)
        z, c = divmod(dp, 2)
        y, x = divmod(t, 4)
        m = 1 if (c == 0) == (step == 0) else 3
        if axis == "x":
            x ^= m
        elif axis == "y":
            y ^= m
        elif axis == "z":
            z ^= m
        else:
            c ^= 1
        out.append((d, (z * 2 + c) * 16 + y * 4 + x))
    return out


def send(a, axis, step=0):
    return lax.ppermute(a, AXES, pairs(axis, step))


def ring_order(me, core):
    first = 1 + 2 * core
    return (me ^ first, me ^ 2, me, me ^ (first ^ 2))


def dot(a, b, dims=None):
    if dims is None:
        return jnp.dot(a, b, preferred_element_type=F32)
    return lax.dot_general(a, b, dims, preferred_element_type=F32)


def gather_cols(ref, lay, r):
    return jnp.concatenate(
        [ref[:, pl.ds(pl.multiple_of(lay[k, r] * BLK, BLK), BLK)] for k in range(KB)], axis=1
    )


def emit_chunks(acc, outer, inner, transposed, sent, stay):
    for p in range(4):
        dst = sent if p < 2 else stay
        for q in range(4):
            y, x = (inner[q], outer[p]) if transposed else (outer[p], inner[q])
            base = (y * 4 + x) * 4
            for j in range(4):
                dst[p % 2, q, :, j * BLK : (j + 1) * BLK] = acc[base + j].astype(BF16)


def main_kernel(
    pos, lin_hbm, lout_hbm, h_hbm, d_hbm, wg_hbm, wu_hbm, wd_hbm,
    keep, give, p_sent, p_stay, q_sent, q_stay, h, d,
    wg, wu, wd, acc_p, acc_q, hid, dgu, turned, lin, lout, sem, w_sem,
):
    small = [
        pltpu.make_async_copy(lin_hbm, lin, sem.at[0]),
        pltpu.make_async_copy(lout_hbm, lout, sem.at[1]),
        pltpu.make_async_copy(h_hbm, h, sem.at[2]),
        pltpu.make_async_copy(d_hbm, d, sem.at[3]),
    ]

    def weights(start, n):
        rows = pl.ds(start * BLK, n * BLK)
        both = ((wg_hbm, wg), (wu_hbm, wu), (wd_hbm, wd))
        return [
            pltpu.make_async_copy(src.at[rows], dst.at[rows], w_sem.at[i, 0 if start == 0 else 1])
            for i, (src, dst) in enumerate(both)
        ]

    early, late = weights(0, EARLY), weights(EARLY, ROWS - EARLY)
    for c in small + early + late:
        c.start()
    acc_p[...] = jnp.zeros_like(acc_p)
    acc_q[...] = jnp.zeros_like(acc_q)
    for c in small + early:
        c.wait()
    z, core = pos[0], pos[1]
    mine = [o * 2 + core for o in ring_order(z, core)]
    others = [o * 2 + 1 - core for o in ring_order(z, 1 - core)]

    def rows_of(r):
        at = r * BLK if isinstance(r, int) else pl.multiple_of(r * BLK, BLK)
        return pl.ds(at, BLK)

    def units(s):
        for i in range(UNROLL):
            r = s * UNROLL + i
            sl = rows_of(r)
            hx, dob = gather_cols(h, lin, r), gather_cols(d, lout, r)
            gate, up, dhid = dot(hx, wg[sl], NT), dot(hx, wu[sl], NT), dot(dob, wd[sl], NT)
            sig = jax.nn.sigmoid(gate)
            silu = gate * sig
            hidden = (silu * up).astype(BF16)
            dgate = (dhid * up * sig * (1.0 + gate * (1.0 - sig))).astype(BF16)
            dup = (dhid * silu).astype(BF16)
            hid[r] = hidden
            dgu[r, :, :BLK] = dgate
            dgu[r, :, BLK:] = dup
            for a, v in enumerate((hidden, dgate, dup)):
                turned[r, a] = v.T.reshape(8, 16, TOK)

    def features(s):
        for i in range(UNROLL):
            r = s * UNROLL + i
            sl = rows_of(r)
            part = dot(hid[r], wd[sl])
            dhx = dot(dgu[r], jnp.concatenate([wg[sl], wu[sl]], axis=0))
            for k in range(KB):
                acc_p[lout[k, r]] += part[:, k * BLK : (k + 1) * BLK]
            for k in range(KB):
                acc_q[lin[k, r]] += dhx[:, k * BLK : (k + 1) * BLK]
            for a in range(3):
                for q in range(4):
                    keep[a, r, q] = turned[r, a, mine[q]]
                    give[a, r, q] = turned[r, a, others[q]]

    units(0)
    for c in late:
        c.wait()
    for s in range(1, ROWS // UNROLL):
        features(s - 1)
        units(s)
    features(ROWS // UNROLL - 1)
    xs, ys = ring_order(pos[3], core), ring_order(pos[2], core)
    emit_chunks(acc_p, xs, ys, True, p_sent, p_stay)
    emit_chunks(acc_q, ys, xs, False, q_sent, q_stay)


def pair_rows(a, b):
    return jnp.concatenate([a, b], axis=0)


def units_of(act0, act1, a, r):
    return jnp.concatenate([act0[a, r].reshape(64, TOK), act1[a, r].reshape(64, TOK)], axis=1)


def grads_kernel(lin, lout, h0, h1, d0, act0, act1, d1_in, keeps, passes, own, after_next, d1, sem):
    copy = pltpu.make_async_copy(d1_in, d1, sem)
    copy.start()

    def put(g, r, rows):
        for q, dst in enumerate((keeps, passes, own, after_next)):
            dst[g, r] = rows[q * 16 : (q + 1) * 16]

    for r in range(ROWS):
        hx = pair_rows(gather_cols(h0, lin, r), gather_cols(h1, lin, r))
        dgu = pair_rows(units_of(act0, act1, 1, r), units_of(act0, act1, 2, r))
        g = dot(dgu, hx).astype(BF16)
        put(0, r, g[:64])
        put(1, r, g[64:])

    copy.wait()

    for r in range(ROWS):
        dob = pair_rows(gather_cols(d0, lout, r), gather_cols(d1, lout, r))
        put(2, r, dot(units_of(act0, act1, 0, r), dob).astype(BF16))


def finish_kernel(own, r1, r2, gate, up, down, tmp):
    for g, out in enumerate((gate, up, down)):
        total = own[g].astype(F32) + r1[g].astype(F32) + r2[g].astype(F32)
        total = total.reshape(ROWS * 16, W)
        for k in range(KB):
            tmp[k] = total[:, k * BLK : (k + 1) * BLK]
        for i in range(16):
            for k in range(KB):
                at = i * W + k * BLK
                out[:, at : at + BLK] = tmp[k, pl.ds(i, ROWS, stride=16), :]


V = pltpu.VMEM
IN_SMEM = pl.BlockSpec(memory_space=pltpu.SMEM)
IN_VMEM = pl.BlockSpec(memory_space=pltpu.VMEM)
ANYWHERE = pl.BlockSpec(memory_space=pl.ANY)
UNROLL = 7
EARLY = 7


def in_hbm(*arrays):
    return [pltpu.with_memory_space_constraint(a, pltpu.HBM) for a in arrays]


def in_vmem(*arrays):
    return [pltpu.with_memory_space_constraint(a, pltpu.VMEM) for a in arrays]


def cost(mib):
    return pl.CostEstimate(flops=0, bytes_accessed=mib * 2**10, transcendentals=0)


def main_call(pos, *arrays):
    act = V((3, ROWS, 4, 16, TOK), BF16)
    chunks = V((2, 4, TOK, W), BF16)
    weight = V((ROWS * BLK, W), BF16)
    total = V((NBLK, TOK, BLK), F32)
    layout = pltpu.SMEM((KB, ROWS), jnp.int32)
    return pl.pallas_call(
        main_kernel,
        in_specs=[IN_SMEM] + [ANYWHERE] * 7,
        out_specs=[IN_VMEM] * 8,
        out_shape=[act, act] + [chunks] * 4 + [V((TOK, D), BF16)] * 2,
        scratch_shapes=[
            weight, weight, weight, total, total,
            V((ROWS, TOK, BLK), BF16), V((ROWS, TOK, 2 * BLK), BF16), V((ROWS, 3, 8, 16, TOK), BF16),
            layout, layout, pltpu.SemaphoreType.DMA((4,)), pltpu.SemaphoreType.DMA((3, 2)),
        ],
        compiler_params=pltpu.CompilerParams(vmem_limit_bytes=24 * 2**20),
        cost_estimate=cost(24),
    )(pos, *in_hbm(*arrays))


GRADS = V((3, ROWS, 16, W), BF16)


def grads_call(lin, lout, h0, h1, d0, act0, act1, d1):
    return pl.pallas_call(
        grads_kernel,
        in_specs=[IN_SMEM] * 2 + [IN_VMEM] * 5 + [ANYWHERE],
        out_specs=[IN_VMEM] * 4,
        out_shape=[GRADS] * 4,
        scratch_shapes=[V((TOK, D), BF16), pltpu.SemaphoreType.DMA],
        compiler_params=pltpu.CompilerParams(vmem_limit_bytes=6 * 2**20),
        cost_estimate=pl.CostEstimate(flops=10**10, bytes_accessed=128 * 2**20, transcendentals=0),
    )(lin, lout, *in_vmem(h0, h1, d0, act0, act1), d1)


def finish_call(*arrays):
    out = jax.ShapeDtypeStruct((ROWS, 16 * W), F32)
    return pl.pallas_call(
        finish_kernel,
        in_specs=[IN_VMEM] * 3,
        out_specs=[IN_VMEM] * 3,
        out_shape=[out] * 3,
        scratch_shapes=[V((KB, ROWS * 16, BLK), F32)],
        compiler_params=pltpu.CompilerParams(vmem_limit_bytes=8 * 2**20),
        cost_estimate=pl.CostEstimate(flops=10**9, bytes_accessed=6 * 2**20, transcendentals=0),
    )(*in_vmem(*arrays))


def add(*terms):
    return sum(t.astype(F32) for t in terms).astype(BF16)


def after(value, other):
    return lax.optimization_barrier((value, other))[0]


def shards(h_in, dout, w_gate, w_up, w_down, in_layout, out_layout):
    in_layout, out_layout = in_layout.T, out_layout.T
    dp, t = lax.axis_index("dp"), lax.axis_index("tensor")
    pos = jnp.stack([dp // 2, dp % 2, t // 4, t % 4]).astype(jnp.int32)
    h_other = send(h_in, "core")
    d_other = send(dout, "core")
    keep, give, p_sent, p_own, q_sent, q_own, h_own, d_own = main_call(
        pos, in_layout, out_layout, h_in, dout, w_gate, w_up, w_down
    )
    taken = send(give, "core")
    p1, q1 = send(p_sent, "x", 0), send(q_sent, "y", 0)
    g_keeps, g_passes, g_own, g_next = grads_call(
        in_layout, out_layout, h_own, h_other, d_own, keep, taken, d_other
    )
    g1 = send(g_passes, "z", 0)
    g1k = send(g_keeps, "z", 0)
    p2 = send(add(p_own[1], p1[1]), "x", 1)
    q2 = send(add(q_own[1], q1[1]), "y", 1)
    g2_in = add(g_next, g1)
    g2 = send(g2_in, "z", 1)
    p_mid = add(p_own[0], p1[0], after(p2, g2_in))
    p3 = send(p_mid[0:2], "y", 0)
    q_mid = add(q_own[0], q1[0], after(q2, p_mid))
    q3 = send(q_mid[0:2], "x", 0)
    p4 = send(add(p_mid[3], p3[1]), "y", 1)
    q4 = send(add(q_mid[3], after(q3, g1k)[1]), "x", 1)
    g_gate, g_up, g_down = finish_call(g_own, g1k, g2)
    out = add(p_mid[2], p3[0], after(p4, g_down))
    dh = add(q_mid[2], q3[0], after(q4, g_down))
    return (out, dh, g_gate, g_up, g_down)


def solution(mesh):
    rows = P("tensor", None)
    return jax.shard_map(
        shards,
        mesh=mesh,
        in_specs=(P("dp", None), P("dp", None), rows, rows, rows, rows, rows),
        out_specs=(P("dp", "tensor"), P("dp", "tensor")) + (P("tensor", "dp"),) * 3,
        check_vma=False,
    )
```

```python
import jax
import jax.numpy as jnp
from jax import lax
from jax.experimental import pallas as pl
from jax.experimental.pallas import tpu as pltpu
from jax.sharding import PartitionSpec as P

D = 8192
BLK = 128
KB = 4
W = KB * BLK
NBLK = D // BLK
ROWS = 14
TOK = 128
AXES = ("dp", "tensor")
F32 = jnp.float32
BF16 = jnp.bfloat16
NT = (((1,), (1,)), ((), ()))


def pairs(axis, step):
    out = []
    for d in range(128):
        dp, t = divmod(d, 16)
        z, c = divmod(dp, 2)
        y, x = divmod(t, 4)
        m = 1 if (c == 0) == (step == 0) else 3
        if axis == "x":
            x ^= m
        elif axis == "y":
            y ^= m
        elif axis == "z":
            z ^= m
        else:
            c ^= 1
        out.append((d, (z * 2 + c) * 16 + y * 4 + x))
    return out


def send(a, axis, step=0):
    return lax.ppermute(a, AXES, pairs(axis, step))


def ring_order(me, core):
    first = 1 + 2 * core
    return (me ^ first, me ^ 2, me, me ^ (first ^ 2))


def dot(a, b, dims=None):
    if dims is None:
        return jnp.dot(a, b, preferred_element_type=F32)
    return lax.dot_general(a, b, dims, preferred_element_type=F32)


def gather_cols(ref, lay, r):
    return jnp.concatenate(
        [ref[:, pl.ds(pl.multiple_of(lay[k, r] * BLK, BLK), BLK)] for k in range(KB)], axis=1
    )


def emit_chunks(acc, outer, inner, transposed, outs):
    for p, dst in enumerate(outs):
        for q in range(4):
            y, x = (inner[q], outer[p]) if transposed else (outer[p], inner[q])
            base = (y * 4 + x) * 4
            for j in range(4):
                dst[q, :, j * BLK : (j + 1) * BLK] = acc[base + j].astype(BF16)


def main_kernel(
    pos, lin_hbm, lout_hbm, h_hbm, d_hbm, wg_hbm, wu_hbm, wd_hbm,
    keep, give, p0, p1, p2, p3, q0, q1, q2, q3, h, d,
    wg, wu, wd, acc_p, acc_q, hid, dgu, turned, lin, lout, sem, w_sem,
):
    small = [
        pltpu.make_async_copy(lin_hbm, lin, sem.at[0]),
        pltpu.make_async_copy(lout_hbm, lout, sem.at[1]),
        pltpu.make_async_copy(h_hbm, h, sem.at[2]),
        pltpu.make_async_copy(d_hbm, d, sem.at[3]),
    ]

    def weights(start, n):
        rows = pl.ds(start * BLK, n * BLK)
        both = ((wg_hbm, wg), (wu_hbm, wu), (wd_hbm, wd))
        return [
            pltpu.make_async_copy(src.at[rows], dst.at[rows], w_sem.at[i, 0 if start == 0 else 1])
            for i, (src, dst) in enumerate(both)
        ]

    early, late = weights(0, EARLY), weights(EARLY, ROWS - EARLY)
    for c in small + early + late:
        c.start()
    acc_p[...] = jnp.zeros_like(acc_p)
    acc_q[...] = jnp.zeros_like(acc_q)
    for c in small + early:
        c.wait()
    z, core = pos[0], pos[1]
    mine = [o * 2 + core for o in ring_order(z, core)]
    others = [o * 2 + 1 - core for o in ring_order(z, 1 - core)]

    def rows_of(r):
        at = r * BLK if isinstance(r, int) else pl.multiple_of(r * BLK, BLK)
        return pl.ds(at, BLK)

    def units(s):
        for i in range(UNROLL):
            r = s * UNROLL + i
            sl = rows_of(r)
            hx, dob = gather_cols(h, lin, r), gather_cols(d, lout, r)
            gate, up, dhid = dot(hx, wg[sl], NT), dot(hx, wu[sl], NT), dot(dob, wd[sl], NT)
            sig = jax.nn.sigmoid(gate)
            silu = gate * sig
            hidden = (silu * up).astype(BF16)
            dgate = (dhid * up * sig * (1.0 + gate * (1.0 - sig))).astype(BF16)
            dup = (dhid * silu).astype(BF16)
            hid[r] = hidden
            dgu[r, :, :BLK] = dgate
            dgu[r, :, BLK:] = dup
            for a, v in enumerate((hidden, dgate, dup)):
                turned[r, a] = v.T.reshape(8, 16, TOK)

    def features(s):
        for i in range(UNROLL):
            r = s * UNROLL + i
            sl = rows_of(r)
            part = dot(hid[r], wd[sl])
            dhx = dot(dgu[r], jnp.concatenate([wg[sl], wu[sl]], axis=0))
            for k in range(KB):
                acc_p[lout[k, r]] += part[:, k * BLK : (k + 1) * BLK]
            for k in range(KB):
                acc_q[lin[k, r]] += dhx[:, k * BLK : (k + 1) * BLK]
            for a in range(3):
                for q in range(4):
                    keep[a, r, q] = turned[r, a, mine[q]]
                    give[a, r, q] = turned[r, a, others[q]]

    units(0)
    for c in late:
        c.wait()
    for s in range(1, ROWS // UNROLL):
        features(s - 1)
        units(s)
    features(ROWS // UNROLL - 1)
    xs, ys = ring_order(pos[3], core), ring_order(pos[2], core)
    emit_chunks(acc_p, xs, ys, True, (p0, p1, p2, p3))
    emit_chunks(acc_q, ys, xs, False, (q0, q1, q2, q3))


def pair_rows(a, b):
    return jnp.concatenate([a, b], axis=0)


def units_of(act0, act1, a, r):
    return jnp.concatenate([act0[a, r].reshape(64, TOK), act1[a, r].reshape(64, TOK)], axis=1)


def grads_kernel(lin, lout, h0, h1, d0, act0, act1, d1_in, keeps, passes, own, after_next, d1, sem):
    copy = pltpu.make_async_copy(d1_in, d1, sem)
    copy.start()

    def put(g, r, rows):
        for q, dst in enumerate((keeps, passes, own, after_next)):
            dst[g, r] = rows[q * 16 : (q + 1) * 16]

    for r in range(ROWS):
        hx = pair_rows(gather_cols(h0, lin, r), gather_cols(h1, lin, r))
        dgu = pair_rows(units_of(act0, act1, 1, r), units_of(act0, act1, 2, r))
        g = dot(dgu, hx).astype(BF16)
        put(0, r, g[:64])
        put(1, r, g[64:])

    copy.wait()

    for r in range(ROWS):
        dob = pair_rows(gather_cols(d0, lout, r), gather_cols(d1, lout, r))
        put(2, r, dot(units_of(act0, act1, 0, r), dob).astype(BF16))


def finish_kernel(own, r1, r2, gate, up, down, tmp):
    for g, out in enumerate((gate, up, down)):
        total = own[g].astype(F32) + r1[g].astype(F32) + r2[g].astype(F32)
        total = total.reshape(ROWS * 16, W)
        for k in range(KB):
            tmp[k] = total[:, k * BLK : (k + 1) * BLK]
        for i in range(16):
            for k in range(KB):
                at = i * W + k * BLK
                out[:, at : at + BLK] = tmp[k, pl.ds(i, ROWS, stride=16), :]


V = pltpu.VMEM
IN_SMEM = pl.BlockSpec(memory_space=pltpu.SMEM)
IN_VMEM = pl.BlockSpec(memory_space=pltpu.VMEM)
ANYWHERE = pl.BlockSpec(memory_space=pl.ANY)
UNROLL = 7
EARLY = 7


def in_hbm(*arrays):
    return [pltpu.with_memory_space_constraint(a, pltpu.HBM) for a in arrays]


def in_vmem(*arrays):
    return [pltpu.with_memory_space_constraint(a, pltpu.VMEM) for a in arrays]


def cost(mib):
    return pl.CostEstimate(flops=0, bytes_accessed=mib * 2**10, transcendentals=0)


def main_call(pos, *arrays):
    act = V((3, ROWS, 4, 16, TOK), BF16)
    chunks = V((4, TOK, W), BF16)
    weight = V((ROWS * BLK, W), BF16)
    total = V((NBLK, TOK, BLK), F32)
    layout = pltpu.SMEM((KB, ROWS), jnp.int32)
    return pl.pallas_call(
        main_kernel,
        in_specs=[IN_SMEM] + [ANYWHERE] * 7,
        out_specs=[IN_VMEM] * 12,
        out_shape=[act, act] + [chunks] * 8 + [V((TOK, D), BF16)] * 2,
        scratch_shapes=[
            weight, weight, weight, total, total,
            V((ROWS, TOK, BLK), BF16), V((ROWS, TOK, 2 * BLK), BF16), V((ROWS, 3, 8, 16, TOK), BF16),
            layout, layout, pltpu.SemaphoreType.DMA((4,)), pltpu.SemaphoreType.DMA((3, 2)),
        ],
        compiler_params=pltpu.CompilerParams(vmem_limit_bytes=24 * 2**20),
        cost_estimate=cost(24),
    )(pos, *in_hbm(*arrays))


GRADS = V((3, ROWS, 16, W), BF16)


def grads_call(lin, lout, h0, h1, d0, act0, act1, d1):
    return pl.pallas_call(
        grads_kernel,
        in_specs=[IN_SMEM] * 2 + [IN_VMEM] * 5 + [ANYWHERE],
        out_specs=[IN_VMEM] * 4,
        out_shape=[GRADS] * 4,
        scratch_shapes=[V((TOK, D), BF16), pltpu.SemaphoreType.DMA],
        compiler_params=pltpu.CompilerParams(vmem_limit_bytes=6 * 2**20),
        cost_estimate=pl.CostEstimate(flops=10**10, bytes_accessed=128 * 2**20, transcendentals=0),
    )(lin, lout, *in_vmem(h0, h1, d0, act0, act1), d1)


def finish_call(*arrays):
    out = jax.ShapeDtypeStruct((ROWS, 16 * W), F32)
    return pl.pallas_call(
        finish_kernel,
        in_specs=[IN_VMEM] * 3,
        out_specs=[IN_VMEM] * 3,
        out_shape=[out] * 3,
        scratch_shapes=[V((KB, ROWS * 16, BLK), F32)],
        compiler_params=pltpu.CompilerParams(vmem_limit_bytes=8 * 2**20),
        cost_estimate=pl.CostEstimate(flops=10**9, bytes_accessed=6 * 2**20, transcendentals=0),
    )(*in_vmem(*arrays))


def add(*terms):
    return sum(t.astype(F32) for t in terms).astype(BF16)


def after(value, other):
    return lax.optimization_barrier((value, other))[0]


def shards(h_in, dout, w_gate, w_up, w_down, in_layout, out_layout):
    in_layout, out_layout = in_layout.T, out_layout.T
    dp, t = lax.axis_index("dp"), lax.axis_index("tensor")
    pos = jnp.stack([dp // 2, dp % 2, t // 4, t % 4]).astype(jnp.int32)
    h_other = send(h_in, "core")
    d_other = send(dout, "core")
    keep, give, p_keeps, p_passes, p_own, p_next, q_keeps, q_passes, q_own, q_next, h_own, d_own = (
        main_call(pos, in_layout, out_layout, h_in, dout, w_gate, w_up, w_down)
    )
    taken = send(give, "core")
    p1, q1 = send(p_passes, "x", 0), send(q_passes, "y", 0)
    p1k, q1k = send(p_keeps, "x", 0), send(q_keeps, "y", 0)
    g_keeps, g_passes, g_own, g_next = grads_call(
        in_layout, out_layout, h_own, h_other, d_own, keep, taken, d_other
    )
    g1 = send(g_passes, "z", 0)
    g1k = send(g_keeps, "z", 0)
    p2 = send(add(p_next, p1), "x", 1)
    q2 = send(add(q_next, q1), "y", 1)
    g2_in = add(g_next, g1)
    g2 = send(g2_in, "z", 1)
    p_mid = add(p_own, p1k, after(p2, g2_in))
    p3 = send(p_mid[0:2], "y", 0)
    q_mid = add(q_own, q1k, after(q2, p_mid))
    q3 = send(q_mid[0:2], "x", 0)
    p4 = send(add(p_mid[3], p3[1]), "y", 1)
    q4 = send(add(q_mid[3], after(q3, g1k)[1]), "x", 1)
    g_gate, g_up, g_down = finish_call(g_own, g1k, g2)
    out = add(p_mid[2], p3[0], after(p4, g_down))
    dh = add(q_mid[2], q3[0], after(q4, g_down))
    return (out, dh, g_gate, g_up, g_down)


def solution(mesh):
    rows = P("tensor", None)
    return jax.shard_map(
        shards,
        mesh=mesh,
        in_specs=(P("dp", None), P("dp", None), rows, rows, rows, rows, rows),
        out_specs=(P("dp", "tensor"), P("dp", "tensor")) + (P("tensor", "dp"),) * 3,
        check_vma=False,
    )
```

```python
import jax
import jax.numpy as jnp
from jax import lax
from jax.experimental import pallas as pl
from jax.experimental.pallas import tpu as pltpu
from jax.sharding import PartitionSpec as P

D = 8192
BLK = 128
KB = 4
W = KB * BLK
NBLK = D // BLK
ROWS = 14
TOK = 128
AXES = ("dp", "tensor")
F32 = jnp.float32
BF16 = jnp.bfloat16
NT = (((1,), (1,)), ((), ()))


def pairs(axis, step):
    out = []
    for d in range(128):
        dp, t = divmod(d, 16)
        z, c = divmod(dp, 2)
        y, x = divmod(t, 4)
        m = 1 if (c == 0) == (step == 0) else 3
        if axis == "x":
            x ^= m
        elif axis == "y":
            y ^= m
        elif axis == "z":
            z ^= m
        else:
            c ^= 1
        out.append((d, (z * 2 + c) * 16 + y * 4 + x))
    return out


def send(a, axis, step=0):
    return lax.ppermute(a, AXES, pairs(axis, step))


def ring_order(me, core):
    first = 1 + 2 * core
    return (me ^ first, me ^ 2, me, me ^ (first ^ 2))


def dot(a, b, dims=None):
    if dims is None:
        return jnp.dot(a, b, preferred_element_type=F32)
    return lax.dot_general(a, b, dims, preferred_element_type=F32)


def gather_cols(ref, lay, r):
    return jnp.concatenate(
        [ref[:, pl.ds(pl.multiple_of(lay[k, r] * BLK, BLK), BLK)] for k in range(KB)], axis=1
    )


def emit_chunks(acc, outer, inner, transposed, outs):
    for p, dst in enumerate(outs):
        for q in range(4):
            y, x = (inner[q], outer[p]) if transposed else (outer[p], inner[q])
            base = (y * 4 + x) * 4
            for j in range(4):
                dst[q, :, j * BLK : (j + 1) * BLK] = acc[base + j].astype(BF16)


def main_kernel(
    pos, lin_hbm, lout_hbm, h_hbm, d_hbm, wg_hbm, wu_hbm, wd_hbm,
    keep, give, p0, p1, p2, p3, q0, q1, q2, q3, h, d,
    wg, wu, wd, acc_p, acc_q, hid, dgu, turned, lin, lout, sem, w_sem,
):
    small = [
        pltpu.make_async_copy(lin_hbm, lin, sem.at[0]),
        pltpu.make_async_copy(lout_hbm, lout, sem.at[1]),
        pltpu.make_async_copy(h_hbm, h, sem.at[2]),
        pltpu.make_async_copy(d_hbm, d, sem.at[3]),
    ]

    def weights(start, n):
        rows = pl.ds(start * BLK, n * BLK)
        both = ((wg_hbm, wg), (wu_hbm, wu), (wd_hbm, wd))
        return [
            pltpu.make_async_copy(src.at[rows], dst.at[rows], w_sem.at[i, 0 if start == 0 else 1])
            for i, (src, dst) in enumerate(both)
        ]

    early, late = weights(0, EARLY), weights(EARLY, ROWS - EARLY)
    for c in small + early + late:
        c.start()
    acc_p[...] = jnp.zeros_like(acc_p)
    acc_q[...] = jnp.zeros_like(acc_q)
    for c in small + early:
        c.wait()
    z, core = pos[0], pos[1]
    mine = [o * 2 + core for o in ring_order(z, core)]
    others = [o * 2 + 1 - core for o in ring_order(z, 1 - core)]

    def rows_of(r):
        at = r * BLK if isinstance(r, int) else pl.multiple_of(r * BLK, BLK)
        return pl.ds(at, BLK)

    def units(s):
        for i in range(UNROLL):
            r = s * UNROLL + i
            sl = rows_of(r)
            hx, dob = gather_cols(h, lin, r), gather_cols(d, lout, r)
            gate, up, dhid = dot(hx, wg[sl], NT), dot(hx, wu[sl], NT), dot(dob, wd[sl], NT)
            sig = jax.nn.sigmoid(gate)
            silu = gate * sig
            hidden = (silu * up).astype(BF16)
            dgate = (dhid * up * sig * (1.0 + gate * (1.0 - sig))).astype(BF16)
            dup = (dhid * silu).astype(BF16)
            hid[r] = hidden
            dgu[r, :, :BLK] = dgate
            dgu[r, :, BLK:] = dup
            for a, v in enumerate((hidden, dgate, dup)):
                turned[r, a] = v.T.reshape(8, 16, TOK)

    def features(s):
        for i in range(UNROLL):
            r = s * UNROLL + i
            sl = rows_of(r)
            part = dot(hid[r], wd[sl])
            dhx = dot(dgu[r], jnp.concatenate([wg[sl], wu[sl]], axis=0))
            for k in range(KB):
                acc_p[lout[k, r]] += part[:, k * BLK : (k + 1) * BLK]
            for k in range(KB):
                acc_q[lin[k, r]] += dhx[:, k * BLK : (k + 1) * BLK]
            for a in range(3):
                for q in range(4):
                    keep[a, r, q] = turned[r, a, mine[q]]
                    give[a, r, q] = turned[r, a, others[q]]

    units(0)
    for c in late:
        c.wait()
    for s in range(1, ROWS // UNROLL):
        features(s - 1)
        units(s)
    features(ROWS // UNROLL - 1)
    xs, ys = ring_order(pos[3], core), ring_order(pos[2], core)
    emit_chunks(acc_p, xs, ys, True, (p0, p1, p2, p3))
    emit_chunks(acc_q, ys, xs, False, (q0, q1, q2, q3))


def pair_rows(a, b):
    return jnp.concatenate([a, b], axis=0)


def units_of(act0, act1, a, r):
    return jnp.concatenate([act0[a, r].reshape(64, TOK), act1[a, r].reshape(64, TOK)], axis=1)


def grads_kernel(lin, lout, h0, h1, d0, d1, act0, act1, keeps, passes, own, after_next):
    def put(g, r, rows):
        for q, dst in enumerate((keeps, passes, own, after_next)):
            dst[g, r] = rows[q * 16 : (q + 1) * 16]

    for r in range(ROWS):
        hx = pair_rows(gather_cols(h0, lin, r), gather_cols(h1, lin, r))
        dgu = pair_rows(units_of(act0, act1, 1, r), units_of(act0, act1, 2, r))
        g = dot(dgu, hx).astype(BF16)
        put(0, r, g[:64])
        put(1, r, g[64:])

    for r in range(ROWS):
        dob = pair_rows(gather_cols(d0, lout, r), gather_cols(d1, lout, r))
        put(2, r, dot(units_of(act0, act1, 0, r), dob).astype(BF16))


def finish_kernel(own, r1, r2, gate, up, down, tmp):
    for g, out in enumerate((gate, up, down)):
        total = own[g].astype(F32) + r1[g].astype(F32) + r2[g].astype(F32)
        total = total.reshape(ROWS * 16, W)
        for k in range(KB):
            tmp[k] = total[:, k * BLK : (k + 1) * BLK]
        for i in range(16):
            for k in range(KB):
                at = i * W + k * BLK
                out[:, at : at + BLK] = tmp[k, pl.ds(i, ROWS, stride=16), :]


V = pltpu.VMEM
IN_SMEM = pl.BlockSpec(memory_space=pltpu.SMEM)
IN_VMEM = pl.BlockSpec(memory_space=pltpu.VMEM)
ANYWHERE = pl.BlockSpec(memory_space=pl.ANY)
UNROLL = 7
EARLY = 7


def in_hbm(*arrays):
    return [pltpu.with_memory_space_constraint(a, pltpu.HBM) for a in arrays]


def in_vmem(*arrays):
    return [pltpu.with_memory_space_constraint(a, pltpu.VMEM) for a in arrays]


def cost(mib):
    return pl.CostEstimate(flops=0, bytes_accessed=mib * 2**10, transcendentals=0)


def main_call(pos, *arrays):
    act = V((3, ROWS, 4, 16, TOK), BF16)
    chunks = V((4, TOK, W), BF16)
    weight = V((ROWS * BLK, W), BF16)
    total = V((NBLK, TOK, BLK), F32)
    layout = pltpu.SMEM((KB, ROWS), jnp.int32)
    return pl.pallas_call(
        main_kernel,
        in_specs=[IN_SMEM] + [ANYWHERE] * 7,
        out_specs=[IN_VMEM] * 12,
        out_shape=[act, act] + [chunks] * 8 + [V((TOK, D), BF16)] * 2,
        scratch_shapes=[
            weight, weight, weight, total, total,
            V((ROWS, TOK, BLK), BF16), V((ROWS, TOK, 2 * BLK), BF16), V((ROWS, 3, 8, 16, TOK), BF16),
            layout, layout, pltpu.SemaphoreType.DMA((4,)), pltpu.SemaphoreType.DMA((3, 2)),
        ],
        compiler_params=pltpu.CompilerParams(vmem_limit_bytes=24 * 2**20),
        cost_estimate=cost(24),
    )(pos, *in_hbm(*arrays))


GRADS = V((3, ROWS, 16, W), BF16)


def grads_call(lin, lout, *arrays):
    return pl.pallas_call(
        grads_kernel,
        in_specs=[IN_SMEM] * 2 + [IN_VMEM] * 6,
        out_specs=[IN_VMEM] * 4,
        out_shape=[GRADS] * 4,
        compiler_params=pltpu.CompilerParams(vmem_limit_bytes=4 * 2**20),
        cost_estimate=pl.CostEstimate(flops=10**10, bytes_accessed=128 * 2**20, transcendentals=0),
    )(lin, lout, *in_vmem(*arrays))


def finish_call(*arrays):
    out = jax.ShapeDtypeStruct((ROWS, 16 * W), F32)
    return pl.pallas_call(
        finish_kernel,
        in_specs=[IN_VMEM] * 3,
        out_specs=[IN_VMEM] * 3,
        out_shape=[out] * 3,
        scratch_shapes=[V((KB, ROWS * 16, BLK), F32)],
        compiler_params=pltpu.CompilerParams(vmem_limit_bytes=8 * 2**20),
        cost_estimate=pl.CostEstimate(flops=10**9, bytes_accessed=6 * 2**20, transcendentals=0),
    )(*in_vmem(*arrays))


def add(*terms):
    return sum(t.astype(F32) for t in terms).astype(BF16)


def after(value, other):
    return lax.optimization_barrier((value, other))[0]


def shards(h_in, dout, w_gate, w_up, w_down, in_layout, out_layout):
    in_layout, out_layout = in_layout.T, out_layout.T
    dp, t = lax.axis_index("dp"), lax.axis_index("tensor")
    pos = jnp.stack([dp // 2, dp % 2, t // 4, t % 4]).astype(jnp.int32)
    h_other = send(h_in, "core")
    d_other = send(dout, "core")
    keep, give, p_keeps, p_passes, p_own, p_next, q_keeps, q_passes, q_own, q_next, h_own, d_own = (
        main_call(pos, in_layout, out_layout, h_in, dout, w_gate, w_up, w_down)
    )
    taken = send(give, "core")
    p1, q1 = send(p_passes, "x", 0), send(q_passes, "y", 0)
    p1k, q1k = send(p_keeps, "x", 0), send(q_keeps, "y", 0)
    g_keeps, g_passes, g_own, g_next = grads_call(
        in_layout, out_layout, h_own, h_other, d_own, d_other, keep, taken
    )
    g1 = send(g_passes, "z", 0)
    g1k = send(g_keeps, "z", 0)
    p2 = send(add(p_next, p1), "x", 1)
    q2 = send(add(q_next, q1), "y", 1)
    g2_in = add(g_next, g1)
    g2 = send(g2_in, "z", 1)
    p_mid = add(p_own, p1k, after(p2, g2_in))
    p3 = send(p_mid[0:2], "y", 0)
    q_mid = add(q_own, q1k, after(q2, p_mid))
    q3 = send(q_mid[0:2], "x", 0)
    p4 = send(add(p_mid[3], p3[1]), "y", 1)
    q4 = send(add(q_mid[3], after(q3, g1k)[1]), "x", 1)
    g_gate, g_up, g_down = finish_call(g_own, g1k, g2)
    out = add(p_mid[2], p3[0], after(p4, g_down))
    dh = add(q_mid[2], q3[0], after(q4, g_down))
    return (out, dh, g_gate, g_up, g_down)


def solution(mesh):
    rows = P("tensor", None)
    return jax.shard_map(
        shards,
        mesh=mesh,
        in_specs=(P("dp", None), P("dp", None), rows, rows, rows, rows, rows),
        out_specs=(P("dp", "tensor"), P("dp", "tensor")) + (P("tensor", "dp"),) * 3,
        check_vma=False,
    )
```

```python
import jax
import jax.numpy as jnp
from jax import lax
from jax.experimental import pallas as pl
from jax.experimental.pallas import tpu as pltpu
from jax.sharding import PartitionSpec as P

D = 8192
BLK = 128
KB = 4
W = KB * BLK
NBLK = D // BLK
ROWS = 14
TOK = 128
AXES = ("dp", "tensor")
F32 = jnp.float32
BF16 = jnp.bfloat16
NT = (((1,), (1,)), ((), ()))


def pairs(axis, step):
    out = []
    for d in range(128):
        dp, t = divmod(d, 16)
        z, c = divmod(dp, 2)
        y, x = divmod(t, 4)
        m = 1 if (c == 0) == (step == 0) else 3
        if axis == "x":
            x ^= m
        elif axis == "y":
            y ^= m
        elif axis == "z":
            z ^= m
        else:
            c ^= 1
        out.append((d, (z * 2 + c) * 16 + y * 4 + x))
    return out


def send(a, axis, step=0):
    return lax.ppermute(a, AXES, pairs(axis, step))


def ring_order(me, core):
    first = 1 + 2 * core
    return (me ^ first, me ^ 2, me, me ^ (first ^ 2))


def dot(a, b, dims=None):
    if dims is None:
        return jnp.dot(a, b, preferred_element_type=F32)
    return lax.dot_general(a, b, dims, preferred_element_type=F32)


def gather_cols(ref, lay, r):
    return jnp.concatenate(
        [ref[:, pl.ds(pl.multiple_of(lay[k, r] * BLK, BLK), BLK)] for k in range(KB)], axis=1
    )


def emit_chunks(acc, outer, inner, transposed, outs):
    for p, dst in enumerate(outs):
        for q in range(4):
            y, x = (inner[q], outer[p]) if transposed else (outer[p], inner[q])
            base = (y * 4 + x) * 4
            for j in range(4):
                dst[q, :, j * BLK : (j + 1) * BLK] = acc[base + j].astype(BF16)


def main_kernel(
    pos, lin_hbm, lout_hbm, h_hbm, d_hbm, wg_hbm, wu_hbm, wd_hbm,
    keep, give, p0, p1, p2, p3, q0, q1, q2, q3, h, d,
    wg, wu, wd, acc_p, acc_q, hid, dgu, turned, lin, lout, sem, w_sem,
):
    small = [
        pltpu.make_async_copy(lin_hbm, lin, sem.at[0]),
        pltpu.make_async_copy(lout_hbm, lout, sem.at[1]),
        pltpu.make_async_copy(h_hbm, h, sem.at[2]),
        pltpu.make_async_copy(d_hbm, d, sem.at[3]),
    ]

    def weights(start, n):
        rows = pl.ds(start * BLK, n * BLK)
        both = ((wg_hbm, wg), (wu_hbm, wu), (wd_hbm, wd))
        return [
            pltpu.make_async_copy(src.at[rows], dst.at[rows], w_sem.at[i, 0 if start == 0 else 1])
            for i, (src, dst) in enumerate(both)
        ]

    early, late = weights(0, EARLY), weights(EARLY, ROWS - EARLY)
    for c in small + early + late:
        c.start()
    acc_p[...] = jnp.zeros_like(acc_p)
    acc_q[...] = jnp.zeros_like(acc_q)
    for c in small + early:
        c.wait()
    z, core = pos[0], pos[1]
    mine = [o * 2 + core for o in ring_order(z, core)]
    others = [o * 2 + 1 - core for o in ring_order(z, 1 - core)]

    def rows_of(r):
        at = r * BLK if isinstance(r, int) else pl.multiple_of(r * BLK, BLK)
        return pl.ds(at, BLK)

    def units(s):
        for i in range(UNROLL):
            r = s * UNROLL + i
            sl = rows_of(r)
            hx, dob = gather_cols(h, lin, r), gather_cols(d, lout, r)
            gate, up, dhid = dot(hx, wg[sl], NT), dot(hx, wu[sl], NT), dot(dob, wd[sl], NT)
            sig = jax.nn.sigmoid(gate)
            silu = gate * sig
            hidden = (silu * up).astype(BF16)
            dgate = (dhid * up * sig * (1.0 + gate * (1.0 - sig))).astype(BF16)
            dup = (dhid * silu).astype(BF16)
            hid[r] = hidden
            dgu[r, :, :BLK] = dgate
            dgu[r, :, BLK:] = dup
            for a, v in enumerate((hidden, dgate, dup)):
                turned[r, a] = v.T.reshape(8, 16, TOK)

    def features(s):
        for i in range(UNROLL):
            r = s * UNROLL + i
            sl = rows_of(r)
            part = dot(hid[r], wd[sl])
            dhx = dot(dgu[r], jnp.concatenate([wg[sl], wu[sl]], axis=0))
            for k in range(KB):
                acc_p[lout[k, r]] += part[:, k * BLK : (k + 1) * BLK]
            for k in range(KB):
                acc_q[lin[k, r]] += dhx[:, k * BLK : (k + 1) * BLK]
            for a in range(3):
                for q in range(4):
                    keep[a, r, q] = turned[r, a, mine[q]]
                    give[a, r, q] = turned[r, a, others[q]]

    units(0)
    for c in late:
        c.wait()
    for s in range(1, ROWS // UNROLL):
        features(s - 1)
        units(s)
    features(ROWS // UNROLL - 1)
    xs, ys = ring_order(pos[3], core), ring_order(pos[2], core)
    emit_chunks(acc_p, xs, ys, True, (p0, p1, p2, p3))
    emit_chunks(acc_q, ys, xs, False, (q0, q1, q2, q3))


def pair_rows(a, b):
    return jnp.concatenate([a, b], axis=0)


def units_of(act0, act1, a, r):
    return jnp.concatenate([act0[a, r].reshape(64, TOK), act1[a, r].reshape(64, TOK)], axis=1)


def grads_kernel(lin, lout, h0, h1, d0, d1, act0, act1, keeps, passes, own, after_next):
    def put(g, r, rows):
        for q, dst in enumerate((keeps, passes, own, after_next)):
            dst[g, r] = rows[q * 16 : (q + 1) * 16]

    for r in range(ROWS):
        hx = pair_rows(gather_cols(h0, lin, r), gather_cols(h1, lin, r))
        dgu = pair_rows(units_of(act0, act1, 1, r), units_of(act0, act1, 2, r))
        g = dot(dgu, hx).astype(BF16)
        put(0, r, g[:64])
        put(1, r, g[64:])

    for r in range(ROWS):
        dob = pair_rows(gather_cols(d0, lout, r), gather_cols(d1, lout, r))
        put(2, r, dot(units_of(act0, act1, 0, r), dob).astype(BF16))


def finish_kernel(own, r1, r2, gate, up, down, tmp):
    for g, out in enumerate((gate, up, down)):
        total = own[g].astype(F32) + r1[g].astype(F32) + r2[g].astype(F32)
        total = total.reshape(ROWS * 16, W)
        for k in range(KB):
            tmp[k] = total[:, k * BLK : (k + 1) * BLK]
        for i in range(16):
            for k in range(KB):
                at = i * W + k * BLK
                out[:, at : at + BLK] = tmp[k, pl.ds(i, ROWS, stride=16), :]


V = pltpu.VMEM
IN_SMEM = pl.BlockSpec(memory_space=pltpu.SMEM)
IN_VMEM = pl.BlockSpec(memory_space=pltpu.VMEM)
ANYWHERE = pl.BlockSpec(memory_space=pl.ANY)
UNROLL = 7
EARLY = 7


def in_hbm(*arrays):
    return [pltpu.with_memory_space_constraint(a, pltpu.HBM) for a in arrays]


def in_vmem(*arrays):
    return [pltpu.with_memory_space_constraint(a, pltpu.VMEM) for a in arrays]


def cost(mib):
    return pl.CostEstimate(flops=0, bytes_accessed=mib * 2**10, transcendentals=0)


def main_call(pos, *arrays):
    act = V((3, ROWS, 4, 16, TOK), BF16)
    chunks = V((4, TOK, W), BF16)
    weight = V((ROWS * BLK, W), BF16)
    total = V((NBLK, TOK, BLK), F32)
    layout = pltpu.SMEM((KB, ROWS), jnp.int32)
    return pl.pallas_call(
        main_kernel,
        in_specs=[IN_SMEM] + [ANYWHERE] * 7,
        out_specs=[IN_VMEM] * 12,
        out_shape=[act, act] + [chunks] * 8 + [V((TOK, D), BF16)] * 2,
        scratch_shapes=[
            weight, weight, weight, total, total,
            V((ROWS, TOK, BLK), BF16), V((ROWS, TOK, 2 * BLK), BF16), V((ROWS, 3, 8, 16, TOK), BF16),
            layout, layout, pltpu.SemaphoreType.DMA((4,)), pltpu.SemaphoreType.DMA((3, 2)),
        ],
        compiler_params=pltpu.CompilerParams(vmem_limit_bytes=24 * 2**20),
        cost_estimate=cost(24),
    )(pos, *in_hbm(*arrays))


GRADS = V((3, ROWS, 16, W), BF16)


def grads_call(lin, lout, *arrays):
    return pl.pallas_call(
        grads_kernel,
        in_specs=[IN_SMEM] * 2 + [IN_VMEM] * 6,
        out_specs=[IN_VMEM] * 4,
        out_shape=[GRADS] * 4,
        compiler_params=pltpu.CompilerParams(vmem_limit_bytes=4 * 2**20),
        cost_estimate=pl.CostEstimate(flops=10**10, bytes_accessed=128 * 2**20, transcendentals=0),
    )(lin, lout, *in_vmem(*arrays))


def finish_call(*arrays):
    out = jax.ShapeDtypeStruct((ROWS, 16 * W), F32)
    return pl.pallas_call(
        finish_kernel,
        in_specs=[IN_VMEM] * 3,
        out_specs=[IN_VMEM] * 3,
        out_shape=[out] * 3,
        scratch_shapes=[V((KB, ROWS * 16, BLK), F32)],
        compiler_params=pltpu.CompilerParams(vmem_limit_bytes=8 * 2**20),
        cost_estimate=pl.CostEstimate(flops=10**9, bytes_accessed=6 * 2**20, transcendentals=0),
    )(*in_vmem(*arrays))


def last_kernel(p_mid, p3, p4, q_mid, q3, q4, out, dh):
    out[...] = add(p_mid[2], p3[0], p4[...])
    dh[...] = add(q_mid[2], q3[0], q4[...])


def last_call(*arrays):
    out = jax.ShapeDtypeStruct((TOK, W), BF16)
    return pl.pallas_call(
        last_kernel,
        in_specs=[IN_VMEM] * 6,
        out_specs=[IN_VMEM] * 2,
        out_shape=[out] * 2,
        compiler_params=pltpu.CompilerParams(vmem_limit_bytes=4 * 2**20),
        cost_estimate=cost(1),
    )(*in_vmem(*arrays))


def add(*terms):
    return sum(t.astype(F32) for t in terms).astype(BF16)


def after(value, other):
    return lax.optimization_barrier((value, other))[0]


def shards(h_in, dout, w_gate, w_up, w_down, in_layout, out_layout):
    in_layout, out_layout = in_layout.T, out_layout.T
    dp, t = lax.axis_index("dp"), lax.axis_index("tensor")
    pos = jnp.stack([dp // 2, dp % 2, t // 4, t % 4]).astype(jnp.int32)
    h_other = send(h_in, "core")
    d_other = send(dout, "core")
    keep, give, p_keeps, p_passes, p_own, p_next, q_keeps, q_passes, q_own, q_next, h_own, d_own = (
        main_call(pos, in_layout, out_layout, h_in, dout, w_gate, w_up, w_down)
    )
    taken = send(give, "core")
    p1, q1 = send(p_passes, "x", 0), send(q_passes, "y", 0)
    p1k, q1k = send(p_keeps, "x", 0), send(q_keeps, "y", 0)
    g_keeps, g_passes, g_own, g_next = grads_call(
        in_layout, out_layout, h_own, h_other, d_own, d_other, keep, taken
    )
    g1 = send(g_passes, "z", 0)
    g1k = send(g_keeps, "z", 0)
    p2 = send(add(p_next, p1), "x", 1)
    q2 = send(add(q_next, q1), "y", 1)
    g2_in = add(g_next, g1)
    g2 = send(g2_in, "z", 1)
    p_mid = add(p_own, p1k, after(p2, g2_in))
    p3 = send(p_mid[0:2], "y", 0)
    q_mid = add(q_own, q1k, after(q2, p_mid))
    q3 = send(q_mid[0:2], "x", 0)
    p4 = send(add(p_mid[3], p3[1]), "y", 1)
    q4 = send(add(q_mid[3], after(q3, g1k)[1]), "x", 1)
    g_gate, g_up, g_down = finish_call(g_own, g1k, g2)
    out, dh = last_call(p_mid, p3, after(p4, g_down), q_mid, q3, q4)
    return (out, dh, g_gate, g_up, g_down)


def solution(mesh):
    rows = P("tensor", None)
    return jax.shard_map(
        shards,
        mesh=mesh,
        in_specs=(P("dp", None), P("dp", None), rows, rows, rows, rows, rows),
        out_specs=(P("dp", "tensor"), P("dp", "tensor")) + (P("tensor", "dp"),) * 3,
        check_vma=False,
    )
```
